32 devices in a mesh: ep: 32 (over z, y, x, core).
Axes of the slice: x: 2, y: 2, z: 4, core: 2. Of those that a mesh axis runs over, the one named last changes fastest.
Arguments:
- tokens: bfloat16 [4096, 2048], P('ep'), may hold values from -6 to 6
- cotangent: bfloat16 [4096, 2048], P('ep'), may hold values from -1 to 1
- gates: float32 [4096, 8], P('ep'), may hold values from 0.1 to 1
- experts: int32 [4096, 8], P('ep'), may hold values from 0 to 31, all different within a row; in each aligned block of 128 rows (0 to 127, 128 to 255, ...) at most 48 rows name the same one
- owner: int32 [32], replicated, may hold values from 0 to 31, each once
- swapped: int32 [16], replicated, may hold values 0 or 1
- w_gate: bfloat16 [32, 2048, 768], P('ep'), may hold values from -0.125 to 0.125
- w_up: bfloat16 [32, 2048, 768], P('ep'), may hold values from -0.125 to 0.125
- w_down: bfloat16 [32, 768, 2048], P('ep'), may hold values from -0.21875 to 0.21875
Outputs:
- mixed: bfloat16 [4096, 2048], P('ep')
- in_grad: bfloat16 [4096, 2048], P('ep')
- gate_grad: float32 [4096, 8], P('ep')
The draws below stay inside these ranges and needn't reach their ends.
Inputs may be any that keep to these rules, and one draw needn't show every extreme that they name: Each row names 8 different experts. In the rows of one device no expert is named by more than 48 rows, and in every draw some expert is named by exactly 48 rows of some device. `owner`: names each device index once.
All inputs are finite; a program needn't handle non-finite values.
Results may differ from the reference program's by a relative error of at most 0.0065.
Values may be sent and summed in bfloat16 or wider, within the bound.
A program may use at most 192 MiB of HBM per device.

```python
import math
import jax
import jax.numpy as jnp
import numpy as np
from jax import lax

D = 2048
FF = 768
TOP = 8
TOK_DEV = 128
EXPERTS = 32
CAP = 48
TOKENS = 4096
PAIRS = 16
N_EP = 32


def plant(drawn, rng, low, high):
    index_at = [jax.random.randint(jax.random.fold_in(rng, axis), (), 0, length) for axis, length in enumerate(drawn.shape)]
    longest = drawn.shape.index(max(drawn.shape))
    next_to = index_at[:longest] + [(index_at[longest] + 1) % drawn.shape[longest]] + index_at[longest + 1:]
    return drawn.at[tuple(index_at)].set(low).at[tuple(next_to)].set(high)


def levels(rng, extent, cuts, least, top_value):
    level = 1.0
    for axis_at, shards_of in cuts:
        heights = jax.random.uniform(jax.random.fold_in(jax.random.fold_in(rng, 6), axis_at), (shards_of,), jnp.float32, least / len(cuts), top_value / len(cuts))
        level = level * jnp.repeat(jnp.exp(heights), extent[axis_at] // shards_of).reshape((-1,) + (1,) * (len(extent) - 1 - axis_at))
    return level


def deal_out(rng, own, number, rows, amount, top, most, lean):
    order = jax.random.permutation(rng, amount)
    crowded, common = portions_of(amount, rows * top, most, lean, True), portions_of(amount, rows * top, most, lean, False)
    places = jnp.arange(amount)

    def named(tallies, rotation):
        used = int((tallies > 0).sum())
        fixed = max(1, used // 4)
        shifted = fixed + (places - fixed + rotation * (used - fixed)) % max(1, amount - fixed)
        return jnp.zeros((amount,), jnp.int32).at[order[jnp.where(places < fixed, places, shifted)]].set(jnp.asarray(tallies, jnp.int32))

    tallies = jnp.where(number % 4 == 0, named(crowded, number // 4), named(common, number - number // 4 - 1))
    mixed = jax.random.permutation(jax.random.fold_in(own, 3), amount)
    source_of, receiver = mixed[0:amount // 2 * 2:2], mixed[1:amount // 2 * 2:2]
    slack = jnp.minimum(tallies[source_of] - 1, most - tallies[receiver]) // 2
    slack = jnp.where((source_of == order[0]) | (receiver == order[0]) | (tallies[receiver] == 0), 0, jnp.maximum(slack, 0))
    shifted = jax.random.randint(jax.random.fold_in(own, 4), (amount // 2,), 0, 1 << 20) % (slack + 1)
    tallies = tallies.at[source_of].add(-shifted).at[receiver].add(shifted)
    labels = jnp.searchsorted(jnp.cumsum(tallies), jnp.arange(rows * top), side="right").astype(jnp.int32)
    grid = labels.reshape(top, rows).T
    grid = grid[jax.random.permutation(jax.random.fold_in(own, 1), rows)]
    rotation = jax.random.randint(jax.random.fold_in(own, 2), (rows, 1), 0, top)
    return jnp.take_along_axis(grid, (jnp.arange(top)[None, :] + rotation) % top, axis=1)


def portions_of(number_of, total, reach, slope, full):
    portions = [(1 << 20) // math.isqrt(grade ** slope) + 1 for grade in range(1, number_of + 1)]
    largest = reach if full else min(reach, max(-(-total // number_of), total * portions[0] // sum(portions)))
    least = 1 if total - largest >= number_of - 1 else 0
    holding, surplus = [largest] + [least] * (number_of - 1), total - largest - least * (number_of - 1)
    while surplus > 0:
        free = [i for i in range(1, number_of) if holding[i] < largest] or [i for i in range(1, number_of) if holding[i] < reach]
        mass, budget = sum([portions[i] for i in free]), surplus
        for i in free:
            extra = min(reach - holding[i], max(1, budget * portions[i] // mass), surplus)
            holding[i] = holding[i] + extra
            surplus = surplus - extra
    return np.array(holding)


def bell_draw(key, extent, scale, bound, cuts=(), held_as=jnp.bfloat16):
    values = scale * jax.random.normal(key, extent, jnp.float32)
    if cuts:
        values = values * levels(key, extent, cuts, -0.22, 0.18)
    return jnp.clip(values, -bound, bound).astype(held_as)


def setup_inputs(seed: int = 0) -> dict:
    key_list = jax.random.split(jax.random.key(seed), 10)
    tokens = bell_draw(key_list[0], (TOKENS, D), 1.0, 6.0, ((0, 32),))
    cotangent = bell_draw(key_list[1], (TOKENS, D), 0.15, 1.0, ((0, 32),))
    gates = jnp.clip(0.1 + 0.9 * jax.random.uniform(key_list[2], (TOKENS, TOP), jnp.float32) ** levels(key_list[2], (TOKENS, TOP), ((0, 32),), -0.2, 0.2), 0.1, 1.0)
    experts_keys = jax.random.split(jax.random.fold_in(key_list[3], 1), TOKENS // TOK_DEV)
    experts_turns = jax.random.permutation(jax.random.fold_in(key_list[3], 3), TOKENS // TOK_DEV)
    experts = jax.vmap(lambda own, number: deal_out(jax.random.fold_in(key_list[3], 2), own, number, TOK_DEV, EXPERTS, TOP, CAP, 2))(experts_keys, experts_turns).reshape((TOKENS, TOP))
    owner = jax.random.permutation(key_list[4], EXPERTS).astype(jnp.int32)
    swapped = plant((jax.random.randint(key_list[5], (PAIRS,), 0, 2) < 1).astype(jnp.int32), jax.random.fold_in(key_list[5], 1), 0, 1)
    w_gate = bell_draw(key_list[6], (EXPERTS, D, FF), D ** -0.5, 0.125, ((0, 32),))
    w_up = bell_draw(key_list[7], (EXPERTS, D, FF), D ** -0.5, 0.125, ((0, 32),))
    w_down = bell_draw(key_list[8], (EXPERTS, FF, D), FF ** -0.5, 0.21875, ((0, 32),))
    return {"tokens": tokens, "cotangent": cotangent, "gates": gates, "experts": experts, "owner": owner, "swapped": swapped, "w_gate": w_gate, "w_up": w_up, "w_down": w_down}


def expert_rows(rows, cots, wg, wu, wd):
    act_a = jnp.dot(rows, wg, preferred_element_type=jnp.float32)
    act_b = jnp.dot(rows, wu, preferred_element_type=jnp.float32)
    sig = jax.nn.sigmoid(act_a)
    hidden = (act_a * sig * act_b).astype(jnp.bfloat16)
    out_rows = jnp.dot(hidden, wd, preferred_element_type=jnp.float32).astype(jnp.bfloat16)
    back_hidden = lax.dot_general(cots, wd, (((1,), (1,)), ((), ())), preferred_element_type=jnp.float32)
    grad_a = (back_hidden * act_b * sig * (1.0 + act_a * (1.0 - sig))).astype(jnp.bfloat16)
    grad_b = (back_hidden * act_a * sig).astype(jnp.bfloat16)
    pair_grad = lax.dot_general(grad_a, wg, (((1,), (1,)), ((), ())), preferred_element_type=jnp.float32)
    pair_grad = pair_grad + lax.dot_general(grad_b, wu, (((1,), (1,)), ((), ())), preferred_element_type=jnp.float32)
    return out_rows, pair_grad.astype(jnp.bfloat16)


def reference(tokens, cotangent, gates, experts, owner, swapped, w_gate, w_up, w_down):
    pairs = TOKENS * TOP
    slab = N_EP * CAP
    flat_e = experts.reshape(-1).astype(jnp.int32)
    planned = owner[flat_e].astype(jnp.int32)
    flag = swapped[planned // 2].astype(jnp.int32)
    target = (planned + flag * (1 - 2 * (planned % 2))).astype(jnp.int32)
    blocks = target.reshape(N_EP, TOK_DEV * TOP)
    hot = (blocks[:, :, None] == jnp.arange(N_EP, dtype=jnp.int32)[None, None, :]).astype(jnp.int32)
    running = jnp.cumsum(hot, axis=1)
    rank = (jnp.sum(hot * running, axis=2) - 1).reshape(-1)
    source_dev = jnp.arange(pairs, dtype=jnp.int32) // (TOK_DEV * TOP)
    place = target * slab + source_dev * CAP + rank
    table = jnp.full((N_EP * slab,), pairs, jnp.int32).at[place].set(jnp.arange(pairs, dtype=jnp.int32))
    tok_pad = jnp.concatenate([tokens, jnp.zeros((1, D), jnp.bfloat16)], axis=0)
    cot_pad = jnp.concatenate([cotangent, jnp.zeros((1, D), jnp.bfloat16)], axis=0)
    gate_pad = jnp.concatenate([gates.reshape(-1), jnp.zeros((1,), jnp.float32)], axis=0)

    def one_device(carry, device):
        mixed_acc, grad_acc, gate_acc = carry
        rows_idx = lax.dynamic_slice_in_dim(table, device * slab, slab)
        token_idx = rows_idx // TOP
        rows = tok_pad[token_idx]
        weight = gate_pad[rows_idx]
        dy_rows = cot_pad[token_idx].astype(jnp.float32)
        cots = (dy_rows * weight[:, None]).astype(jnp.bfloat16)
        out_rows, pair_grad = expert_rows(rows, cots, w_gate[device], w_up[device], w_down[device])
        out_f = out_rows.astype(jnp.float32)
        mixed_acc = mixed_acc.at[token_idx].add(weight[:, None] * out_f, mode="drop")
        grad_acc = grad_acc.at[token_idx].add(pair_grad.astype(jnp.float32), mode="drop")
        gate_acc = gate_acc.at[rows_idx].set(jnp.sum(dy_rows * out_f, axis=1), mode="drop")
        return (mixed_acc, grad_acc, gate_acc), None

    start = (jnp.zeros((TOKENS, D), jnp.float32), jnp.zeros((TOKENS, D), jnp.float32), jnp.zeros((pairs,), jnp.float32))
    final, _ = lax.scan(one_device, start, jnp.arange(N_EP, dtype=jnp.int32))
    mixed_acc, grad_acc, gate_acc = final
    return mixed_acc.astype(jnp.bfloat16), grad_acc.astype(jnp.bfloat16), gate_acc.reshape(TOKENS, TOP)
```

```python
import jax
import jax.numpy as jnp
from jax import lax
from jax.sharding import PartitionSpec as P


def body(tokens, cotangent, gates, experts, owner, swapped, w_gate, w_up, w_down):
    tok_rows, width = tokens.shape
    top_count = experts.shape[1]
    expert_total = owner.shape[0]
    count = lax.axis_size("ep")
    slots = tok_rows * top_count * 3 // (2 * expert_total)
    f32, bf16 = jnp.float32, jnp.bfloat16
    devices = jnp.arange(count, dtype=jnp.int32)
    dev_flag = jnp.repeat(swapped, 2)
    step_dev = dev_flag * (1 - 2 * (devices % 2))
    holder = owner + jnp.sum(
        jnp.where(owner[:, None] == devices[None, :], step_dev[None, :], 0), axis=1
    )
    wg, wu, wd = w_gate[0], w_up[0], w_down[0]
    tok_all = lax.all_gather(tokens, "ep", axis=0, tiled=False)
    cot_all = lax.all_gather(cotangent, "ep", axis=0, tiled=False)
    held = jnp.sum(
        jnp.where(holder[None, :] == devices[:, None], jnp.arange(expert_total, dtype=jnp.int32)[None, :], 0),
        axis=1,
    )
    hit = experts[None, :, :] == held[:, None, None]
    weight = jnp.sum(jnp.where(hit, gates[None, :, :], 0.0), axis=2)
    weight = lax.all_to_all(weight, "ep", split_axis=0, concat_axis=0, tiled=True)
    mask = weight > 0.0
    at = jnp.arange(tok_rows, dtype=jnp.int32)
    before = (at[:, None] < at[None, :]).astype(bf16)
    rank = jnp.dot(mask.astype(bf16), before, preferred_element_type=f32).astype(jnp.int32)
    rank = jnp.where(mask, rank, -1)
    pick = rank[:, None, :] == jnp.arange(slots, dtype=jnp.int32)[None, :, None]
    w_rows = jnp.sum(jnp.where(pick, weight[:, None, :], 0.0), axis=2).reshape(-1, 1)
    pick = pick.astype(bf16)

    def gather(x):
        return lax.dot_general(
            pick, x, (((2,), (1,)), ((0,), (0,))), preferred_element_type=f32
        ).astype(bf16).reshape(-1, width)

    def spread(rows):
        return lax.dot_general(
            pick, rows.reshape(count, slots, width), (((1,), (1,)), ((0,), (0,))), preferred_element_type=f32
        ).astype(bf16)

    x = gather(tok_all)
    c = gather(cot_all)
    a = jnp.dot(x, wg, preferred_element_type=f32)
    b = jnp.dot(x, wu, preferred_element_type=f32)
    sig = jax.nn.sigmoid(a)
    hidden = (a * sig * b).astype(bf16)
    out = jnp.dot(hidden, wd, preferred_element_type=f32).astype(bf16).astype(f32)
    mixed = spread((w_rows * out).astype(bf16))
    mixed = lax.psum_scatter(mixed, "ep", scatter_dimension=0, tiled=False)
    cf = c.astype(f32)
    gg = jnp.sum(cf * out, axis=1).reshape(count, slots)
    gg = jnp.sum(jnp.where(pick > 0, gg[:, :, None], 0.0), axis=1)
    gg = lax.all_to_all(gg, "ep", split_axis=0, concat_axis=0, tiled=True)
    gate_grad = jnp.sum(jnp.where(hit, gg[:, :, None], 0.0), axis=0)
    cs = (cf * w_rows).astype(bf16)
    bh = lax.dot_general(cs, wd, (((1,), (1,)), ((), ())), preferred_element_type=f32)
    ga = (bh * b * sig * (1.0 + a * (1.0 - sig))).astype(bf16)
    gb = (bh * a * sig).astype(bf16)
    pg = lax.dot_general(ga, wg, (((1,), (1,)), ((), ())), preferred_element_type=f32)
    pg = pg + lax.dot_general(gb, wu, (((1,), (1,)), ((), ())), preferred_element_type=f32)
    in_grad = lax.psum_scatter(spread(pg.astype(bf16)), "ep", scatter_dimension=0, tiled=False)
    return (mixed, in_grad, gate_grad)


def solution(mesh):
    return jax.shard_map(
        body,
        mesh=mesh,
        in_specs=(
            P("ep", None),
            P("ep", None),
            P("ep", None),
            P("ep", None),
            P(),
            P(),
            P("ep", None, None),
            P("ep", None, None),
            P("ep", None, None),
        ),
        out_specs=(P("ep", None), P("ep", None), P("ep", None)),
        check_vma=False,
    )
```

```python
import functools

import jax
import jax.numpy as jnp
from jax import lax
from jax.experimental import pallas as pl
from jax.experimental.pallas import tpu as pltpu
from jax.sharding import PartitionSpec as P

NZ = 4
MESH = pl.DeviceIdType.MESH


def places():
    me = lax.axis_index("ep")
    return me // 8, lax.rem(me // 4, 2), lax.rem(me // 2, 2), lax.rem(me, 2)


def at_place(z, y, x, c):
    return ((z * 2 + y) * 2 + x) * 2 + c


def greet(peers):
    barrier = pltpu.get_barrier_semaphore()
    for peer in peers:
        pl.semaphore_signal(barrier, inc=1, device_id=(peer,), device_id_type=MESH)
    pl.semaphore_wait(barrier, len(peers))


def gather_kernel(n, *refs):
    ins, outs = refs[:n], refs[n : 2 * n]
    send, recv, local = refs[2 * n :]
    z, y, x, c = places()
    rows = ins[0].shape[0]
    half = rows // 2
    me = at_place(z, y, x, c)
    xp, yp = at_place(z, y, 1 - x, c), at_place(z, 1 - y, x, c)
    sib = at_place(z, y, x, 1 - c)

    def zi(d):
        return lax.rem(z + NZ + d, NZ)

    zp = {d: at_place(zi(d), y, x, c) for d in (1, 2, 3)}
    greet([zp[1], zp[2], zp[3], xp, yp, sib])

    def origin(q, d, core):
        return at_place(zi(-d), 1 - y if "y" in q else y, 1 - x if "x" in q else x, core)

    def copy(t, role, where, cut, dev, own=False):
        src = ins[t] if own else outs[t].at[where]
        dst = outs[t].at[where]
        if cut is not None:
            src, dst = src.at[pl.ds(cut * half, half)], dst.at[pl.ds(cut * half, half)]
        return pltpu.make_async_remote_copy(
            src_ref=src,
            dst_ref=dst,
            send_sem=send.at[t, role],
            recv_sem=recv.at[t, role],
            device_id=(dev,),
            device_id_type=MESH,
        )

    Z, Y, X, XY, YX, S = 0, 4, 8, 12, 16, 20
    Q = {"o": 0, "y": 4, "x": 8, "xy": 12}
    sent = []

    def go(*args, **kw):
        cp = copy(*args, **kw)
        cp.start()
        sent.append(cp)

    def to_sib(t, q, d):
        go(t, S + Q[q] + d, origin(q, d, c), None, sib, own=(q == "o" and d == 0))

    def arrived(t, role, where, cut=None):
        copy(t, role, where, cut, sib).wait_recv()

    locals_ = []
    for t in range(n):
        for d in (2, 1, 3):
            go(t, Z + d, me, None, zp[d], own=True)
        go(t, Y, me, None, yp, own=True)
        go(t, X, me, None, xp, own=True)
        to_sib(t, "o", 0)
        cp = pltpu.make_async_copy(ins[t], outs[t].at[me], local.at[t])
        cp.start()
        locals_.append(cp)
    for t in range(n):
        for d in (0, 1, 3, 2):
            if d:
                arrived(t, Z + d, origin("o", d, c))
                go(t, Y + d, origin("o", d, c), None, yp)
                go(t, X + d, origin("o", d, c), None, xp)
                to_sib(t, "o", d)
        for d in (0, 1, 3, 2):
            arrived(t, Y + d, origin("y", d, c))
            go(t, XY + d, origin("y", d, c), 0, xp)
            to_sib(t, "y", d)
            arrived(t, X + d, origin("x", d, c))
            go(t, YX + d, origin("x", d, c), 1, yp)
            to_sib(t, "x", d)
    for t in range(n):
        for d in (0, 1, 3, 2):
            arrived(t, XY + d, origin("xy", d, c), 0)
            arrived(t, YX + d, origin("xy", d, c), 1)
            to_sib(t, "xy", d)
    for t in range(n):
        for q in Q:
            for d in range(NZ):
                arrived(t, S + Q[q] + d, origin(q, d, 1 - c))
    for cp in locals_:
        cp.wait()
    for cp in sent:
        cp.wait_send()


def gather_blocks(*xs):
    n = len(xs)
    count = lax.axis_size("ep")
    if count != 32:
        return [lax.all_gather(v, "ep", axis=0, tiled=False) for v in xs]
    return pl.pallas_call(
        functools.partial(gather_kernel, n),
        out_shape=[jax.ShapeDtypeStruct((count,) + v.shape, v.dtype) for v in xs],
        in_specs=[pl.BlockSpec(memory_space=pl.ANY)] * n,
        out_specs=[pl.BlockSpec(memory_space=pl.ANY)] * n,
        scratch_shapes=[
            pltpu.SemaphoreType.DMA((n, 36)),
            pltpu.SemaphoreType.DMA((n, 36)),
            pltpu.SemaphoreType.DMA((n,)),
        ],
        compiler_params=pltpu.CompilerParams(collective_id=0, has_side_effects=True),
        cost_estimate=pl.CostEstimate(flops=0, bytes_accessed=n * 32 * xs[0].size * 2, transcendentals=0),
    )(*xs)


def scatter_kernel(n, *refs):
    ins, outs = refs[:n], refs[n : 2 * n]
    acc, r0, r1, r2, r3, send, recv, local = refs[2 * n :]
    z, y, x, c = places()
    rows, width = outs[0].shape
    half = rows // 2
    step = 16
    f32 = jnp.float32
    xp, yp = at_place(z, y, 1 - x, c), at_place(z, 1 - y, x, c)
    sib = at_place(z, y, x, 1 - c)

    def zi(d):
        return lax.rem(z + d, NZ)

    zp = {d: at_place(zi(d), y, x, c) for d in (1, 2, 3)}
    greet([zp[1], zp[2], zp[3], xp, yp, sib])
    Q = {"o": 0, "y": 4, "x": 8, "xy": 12}
    A1, A2, Z = 16, 32, 40

    def block(q, d, core):
        return at_place(zi(d), 1 - y if "y" in q else y, 1 - x if "x" in q else x, core)

    def copy(t, role, src, dst, dev):
        return pltpu.make_async_remote_copy(
            src_ref=src,
            dst_ref=dst,
            send_sem=send.at[t, role],
            recv_sem=recv.at[t, role],
            device_id=(dev,),
            device_id_type=MESH,
        )

    sent = []

    def go(*args):
        cp = copy(*args)
        cp.start()
        sent.append(cp)

    def arrived(t, role, dst, dev):
        copy(t, role, dst, dst, dev).wait_recv()

    def add(dst, terms, lo, size):
        @pl.loop(0, size // step)
        def _(i):
            at = pl.ds(pl.multiple_of(lo + i * step, step), step)
            there = pl.ds(pl.multiple_of(i * step, step), step)
            total = None
            for term, whole in terms:
                v = term[at if whole else there, :].astype(f32)
                total = v if total is None else total + v
            dst[at, :] = total.astype(dst.dtype)

    order = [(t, d) for t in range(n) for d in (2, 1, 3, 0)]
    for t, d in order:
        for q in ("xy", "x", "y", "o"):
            go(t, Q[q] + d, ins[t].at[block(q, d, 1 - c)], r0.at[t, Q[q] + d], sib)
            pltpu.make_async_copy(ins[t].at[block(q, d, c)], acc.at[t, Q[q] + d], local.at[t, Q[q] + d]).start()

    def stage0(t, d):
        for q in ("xy", "x", "y", "o"):
            s = Q[q] + d
            pltpu.make_async_copy(ins[t].at[block(q, d, c)], acc.at[t, s], local.at[t, s]).wait()
            arrived(t, s, r0.at[t, s], sib)
            add(acc.at[t, s], [(acc.at[t, s], True), (r0.at[t, s], True)], 0, rows)
            first, second = acc.at[t, s, pl.ds(0, half)], acc.at[t, s, pl.ds(half, half)]
            if q == "xy":
                go(t, A1 + 4 + d, first, r1.at[t, 4 + d], xp)
                go(t, A1 + 12 + d, second, r1.at[t, 12 + d], yp)
            elif q == "x":
                go(t, A1 + d, first, r1.at[t, d], xp)
            elif q == "y":
                go(t, A1 + 8 + d, second, r1.at[t, 8 + d], yp)

    def stage1(t, d):
        sy, sx = Q["y"] + d, Q["x"] + d
        arrived(t, A1 + 4 + d, r1.at[t, 4 + d], xp)
        add(acc.at[t, sy], [(acc.at[t, sy], True), (r1.at[t, 4 + d], False)], 0, half)
        go(t, A2 + d, acc.at[t, sy, pl.ds(0, half)], r2.at[t, d], yp)
        arrived(t, A1 + 12 + d, r1.at[t, 12 + d], yp)
        add(acc.at[t, sx], [(acc.at[t, sx], True), (r1.at[t, 12 + d], False)], half, half)
        go(t, A2 + 4 + d, acc.at[t, sx, pl.ds(half, half)], r2.at[t, 4 + d], xp)

    def stage2(t, d):
        arrived(t, A1 + d, r1.at[t, d], xp)
        arrived(t, A2 + d, r2.at[t, d], yp)
        add(acc.at[t, d], [(acc.at[t, d], True), (r1.at[t, d], False), (r2.at[t, d], False)], 0, half)
        arrived(t, A1 + 8 + d, r1.at[t, 8 + d], yp)
        arrived(t, A2 + 4 + d, r2.at[t, 4 + d], xp)
        add(acc.at[t, d], [(acc.at[t, d], True), (r1.at[t, 8 + d], False), (r2.at[t, 4 + d], False)], half, half)
        if d:
            go(t, Z + d, acc.at[t, d], r3.at[t, d - 1], zp[d])

    for k in range(len(order) + 2):
        if k < len(order):
            stage0(*order[k])
        if 1 <= k < len(order) + 1:
            stage1(*order[k - 1])
        if k >= 2:
            stage2(*order[k - 2])
    for t in range(n):
        for d in (1, 2, 3):
            arrived(t, Z + d, r3.at[t, d - 1], zp[d])
        add(outs[t], [(acc.at[t, 0], True)] + [(r3.at[t, d], True) for d in range(3)], 0, rows)
    for cp in sent:
        cp.wait_send()


def scatter_sums(*xs):
    n = len(xs)
    count, rows, width = xs[0].shape
    if count != 32:
        return [lax.psum_scatter(v, "ep", scatter_dimension=0, tiled=False) for v in xs]
    bf16 = jnp.bfloat16
    return pl.pallas_call(
        functools.partial(scatter_kernel, n),
        out_shape=[jax.ShapeDtypeStruct((rows, width), bf16) for v in xs],
        in_specs=[pl.BlockSpec(memory_space=pl.ANY)] * n,
        out_specs=[pl.BlockSpec(memory_space=pltpu.VMEM)] * n,
        scratch_shapes=[
            pltpu.VMEM((n, 16, rows, width), bf16),
            pltpu.VMEM((n, 16, rows, width), bf16),
            pltpu.VMEM((n, 16, rows // 2, width), bf16),
            pltpu.VMEM((n, 8, rows // 2, width), bf16),
            pltpu.VMEM((n, 3, rows, width), bf16),
            pltpu.SemaphoreType.DMA((n, 44)),
            pltpu.SemaphoreType.DMA((n, 44)),
            pltpu.SemaphoreType.DMA((n, 16)),
        ],
        compiler_params=pltpu.CompilerParams(
            collective_id=1, has_side_effects=True, vmem_limit_bytes=58 << 20
        ),
        cost_estimate=pl.CostEstimate(flops=0, bytes_accessed=n * 32 * rows * width * 2, transcendentals=0),
    )(*xs)


def body(tokens, cotangent, gates, experts, owner, swapped, w_gate, w_up, w_down):
    tok_rows, width = tokens.shape
    top_count = experts.shape[1]
    expert_total = owner.shape[0]
    count = lax.axis_size("ep")
    slots = tok_rows * top_count * 3 // (2 * expert_total)
    f32, bf16 = jnp.float32, jnp.bfloat16
    devices = jnp.arange(count, dtype=jnp.int32)
    dev_flag = jnp.repeat(swapped, 2)
    step_dev = dev_flag * (1 - 2 * (devices % 2))
    holder = owner + jnp.sum(
        jnp.where(owner[:, None] == devices[None, :], step_dev[None, :], 0), axis=1
    )
    wg, wu, wd = w_gate[0], w_up[0], w_down[0]
    tok_all, cot_all = gather_blocks(tokens, cotangent)
    held = jnp.sum(
        jnp.where(holder[None, :] == devices[:, None], jnp.arange(expert_total, dtype=jnp.int32)[None, :], 0),
        axis=1,
    )
    hit = experts[None, :, :] == held[:, None, None]
    weight = jnp.sum(jnp.where(hit, gates[None, :, :], 0.0), axis=2)
    weight = lax.all_to_all(weight, "ep", split_axis=0, concat_axis=0, tiled=True)
    mask = weight > 0.0
    at = jnp.arange(tok_rows, dtype=jnp.int32)
    before = (at[:, None] < at[None, :]).astype(bf16)
    rank = jnp.dot(mask.astype(bf16), before, preferred_element_type=f32).astype(jnp.int32)
    rank = jnp.where(mask, rank, -1)
    pick = rank[:, None, :] == jnp.arange(slots, dtype=jnp.int32)[None, :, None]
    w_rows = jnp.sum(jnp.where(pick, weight[:, None, :], 0.0), axis=2).reshape(-1, 1)
    pick = pick.astype(bf16)

    def gather(x):
        return lax.dot_general(
            pick, x, (((2,), (1,)), ((0,), (0,))), preferred_element_type=f32
        ).astype(bf16).reshape(-1, width)

    def spread(rows):
        return lax.dot_general(
            pick, rows.reshape(count, slots, width), (((1,), (1,)), ((0,), (0,))), preferred_element_type=f32
        ).astype(bf16)

    x = gather(tok_all)
    c = gather(cot_all)
    a = jnp.dot(x, wg, preferred_element_type=f32)
    b = jnp.dot(x, wu, preferred_element_type=f32)
    sig = jax.nn.sigmoid(a)
    hidden = (a * sig * b).astype(bf16)
    out = jnp.dot(hidden, wd, preferred_element_type=f32).astype(bf16).astype(f32)
    mixed = spread((w_rows * out).astype(bf16))
    cf = c.astype(f32)
    gg = jnp.sum(cf * out, axis=1).reshape(count, slots)
    gg = jnp.sum(jnp.where(pick > 0, gg[:, :, None], 0.0), axis=1)
    gg = lax.all_to_all(gg, "ep", split_axis=0, concat_axis=0, tiled=True)
    gate_grad = jnp.sum(jnp.where(hit, gg[:, :, None], 0.0), axis=0)
    cs = (cf * w_rows).astype(bf16)
    bh = lax.dot_general(cs, wd, (((1,), (1,)), ((), ())), preferred_element_type=f32)
    ga = (bh * b * sig * (1.0 + a * (1.0 - sig))).astype(bf16)
    gb = (bh * a * sig).astype(bf16)
    pg = lax.dot_general(ga, wg, (((1,), (1,)), ((), ())), preferred_element_type=f32)
    pg = pg + lax.dot_general(gb, wu, (((1,), (1,)), ((), ())), preferred_element_type=f32)
    mixed, in_grad = scatter_sums(mixed, spread(pg.astype(bf16)))
    return (mixed, in_grad, gate_grad)


def solution(mesh):
    return jax.shard_map(
        body,
        mesh=mesh,
        in_specs=(
            P("ep", None),
            P("ep", None),
            P("ep", None),
            P("ep", None),
            P(),
            P(),
            P("ep", None, None),
            P("ep", None, None),
            P("ep", None, None),
        ),
        out_specs=(P("ep", None), P("ep", None), P("ep", None)),
        check_vma=False,
    )
```
